32 devices in a mesh: grp: 2 (over x), row: 16 (over z, y, core).
Axes of the slice: x: 2, y: 2, z: 4, core: 2. Of those that a mesh axis runs over, the one named last changes fastest.
Arguments:
- prints_a: int32 [5120, 4], P(('grp', 'row')), parts along dimension 0, may hold values from 0 to 1073741823, as said below
- prints_b: int32 [5120, 4], P(('grp', 'row')), parts along dimension 0, may hold values from 0 to 1073741823, as said below
- prints_c: int32 [5120, 4], P(('grp', 'row')), parts along dimension 0, may hold values from 0 to 1073741823, as said below
- prints_d: int32 [5120, 4], P(('grp', 'row')), parts along dimension 0, may hold values from 0 to 1073741823, as said below
- start_block: float32 [5120, 64], P(('grp', 'row')), parts along dimension 0, may hold values from -6 to 6
Outputs:
- basis: float32 [5120, 64], P(('grp', 'row')), parts along dimension 0
The draws below stay inside these ranges and needn't reach their ends.
There are 2 independent parts, one for each index of `grp`. The reference program is written for one: setup_inputs(seed, part) draws one part's arguments, and reference() takes and returns one part's arrays. A program takes and returns all parts, laid end to end along the dimension named above; each array names one. Nothing has to cross between parts.
Inputs may be any that keep to these rules, and one draw needn't show every extreme that they name: `prints_a`: every word lies below 2 to the 30th and word 0 of every molecule is nonzero, so every fingerprint has a set bit. `prints_b`: every word lies below 2 to the 30th. `prints_c`: every word lies below 2 to the 30th. `prints_d`: every word lies below 2 to the 30th.
All inputs are finite; a program needn't handle non-finite values.
Results may differ from the reference program's by a relative error of at most 0.0003.
Values sent between devices are 32-bit elements; how exact they have to be, the bound alone decides.
A program may use at most 128 MiB of HBM per device.

```python
import math
import jax
import jax.numpy as jnp
from jax import lax

ROWS = 160
BLOCK = 64
STEPS = 2
WORDS_PART = 4
MOLS = 2560


top_value = 1073741824


def density_of(key):
    return jax.random.randint(jax.random.fold_in(key, 7), (MOLS, 1), 0, 4, dtype=jnp.int32)


def draw_words(key, salt):
    shape = (MOLS, WORDS_PART)
    words = jax.random.randint(jax.random.fold_in(key, 100 + salt), shape, 0, top_value, dtype=jnp.int32)
    density_level = density_of(key)
    for repeat_index in range(3):
        mask_word = jax.random.randint(jax.random.fold_in(key, 200 + 10 * salt + repeat_index), shape, 0, top_value, dtype=jnp.int32)
        words = jnp.where(density_level > repeat_index, jnp.bitwise_and(words, mask_word), words)
    words = words.at[0, 1].set(top_value - 1)
    words = words.at[1, WORDS_PART - 1].set(0)
    return words


def draw_prints_a(key, part):
    words = draw_words(key, 0)
    position = jax.random.randint(jax.random.fold_in(key, 300), (MOLS,), 0, 30, dtype=jnp.int32)
    first_word = jnp.bitwise_or(words[:, 0], jnp.left_shift(jnp.ones((MOLS,), jnp.int32), position))
    return words.at[:, 0].set(first_word)


def draw_prints_b(key, part):
    return draw_words(key, 1)


def draw_prints_c(key, part):
    return draw_words(key, 2)


def draw_prints_d(key, part):
    return draw_words(key, 3)


def shard_levels(own_key, dims, pieces, low, high):
    level = 1.0
    for dim, shards_of in pieces:
        steps = jax.random.uniform(jax.random.fold_in(jax.random.fold_in(own_key, 6), dim), (shards_of,), jnp.float32, low / len(pieces), high / len(pieces))
        level = level * jnp.repeat(jnp.exp(steps), dims[dim] // shards_of).reshape((-1,) + (1,) * (len(dims) - 1 - dim))
    return level


def gaussian(stream_key, dims, spread, most, cuts=(), held_as=jnp.bfloat16):
    entries = jax.random.normal(stream_key, dims, jnp.float32) * spread
    if len(cuts) > 0:
        entries = shard_levels(stream_key, dims, cuts, -0.22, 0.18) * entries
    return jnp.clip(entries, min=-most, max=most).astype(held_as)


def setup_inputs(seed: int = 0, part: int = 0) -> dict:
    seeds = jax.random.split(jax.random.key(seed), 6)
    part_keys = jax.random.split(jax.random.fold_in(seeds[5], part), 6)
    prints_a = draw_prints_a(jax.random.fold_in(jax.random.fold_in(seeds[5], part), 71), part)
    prints_b = draw_prints_b(jax.random.fold_in(jax.random.fold_in(seeds[5], part), 71), part)
    prints_c = draw_prints_c(jax.random.fold_in(jax.random.fold_in(seeds[5], part), 71), part)
    prints_d = draw_prints_d(jax.random.fold_in(jax.random.fold_in(seeds[5], part), 71), part)
    start_block = gaussian(part_keys[4], (MOLS, BLOCK), 1.0, 6.0, ((0, 16),), jnp.float32)
    return dict(prints_a=prints_a, prints_b=prints_b, prints_c=prints_c, prints_d=prints_d, start_block=start_block)


def unpack(words):
    shifts = jnp.arange(30, dtype=jnp.int32)
    expanded = jnp.bitwise_and(jnp.right_shift(words[:, :, None], shifts[None, None, :]), 1)
    return expanded.reshape(words.shape[0], -1).astype(jnp.bfloat16)

def tanimoto(bits_left, count_left, bits_right, count_right):
    shared = jnp.dot(bits_left.astype(jnp.float32), bits_right.T.astype(jnp.float32), precision=lax.Precision.HIGHEST, preferred_element_type=jnp.float32)
    return shared / (count_left[:, None] + count_right[None, :] - shared)

def reference(prints_a, prints_b, prints_c, prints_d, start_block):
    words = jnp.concatenate([prints_a, prints_b, prints_c, prints_d], axis=1)
    bits = unpack(words).astype(jnp.float32)
    ones_count = lax.optimization_barrier(jnp.sum(bits, axis=1))
    bit_blocks = bits.reshape(MOLS // ROWS, ROWS, -1)
    count_blocks = ones_count.reshape(MOLS // ROWS, ROWS)

    def kernel_times(operand):

        def one_block(pair):
            tile_rows = tanimoto(pair[0], pair[1], bits, ones_count)
            return jnp.dot(tile_rows.astype(jnp.float32), operand.astype(jnp.float32), precision=lax.Precision.HIGHEST, preferred_element_type=jnp.float32)
        return lax.map(one_block, (bit_blocks, count_blocks)).reshape(MOLS, -1)
    degree = kernel_times(jnp.ones((MOLS, 1), jnp.float32))[:, 0]
    volume = jnp.sum(degree)
    root = jnp.sqrt(degree)
    block = start_block
    for step_index in range(STEPS):
        scaled = block / root[:, None]
        reach = kernel_times(scaled)
        proj = lax.optimization_barrier(jnp.sum(root[:, None] * block, axis=0))
        image = reach / root[:, None] - root[:, None] * (proj / volume)[None, :]
        gram = jnp.dot(image.T.astype(jnp.float32), image.astype(jnp.float32), precision=lax.Precision.HIGHEST, preferred_element_type=jnp.float32)
        factor = jnp.linalg.cholesky(gram)
        block = lax.linalg.triangular_solve(factor, image, left_side=False, lower=True, transpose_a=True)
    return (block * math.sqrt(MOLS)).astype(jnp.float32)
```

```python
import functools
import math

import jax
import jax.numpy as jnp
from jax import lax
from jax.experimental import pallas as pl
from jax.experimental.pallas import tpu as pltpu
from jax.sharding import PartitionSpec as P

F32 = jnp.float32
BF16 = jnp.bfloat16
HIGHEST = lax.Precision.HIGHEST
MESH = pl.DeviceIdType.MESH


def dot(left, right, dims, precision=None):
    return lax.dot_general(
        left, right, ((dims[:1], dims[1:]), ((), ())),
        precision=precision, preferred_element_type=F32,
    )


def swap(value):
    return pltpu.roll(value, 64, 1)


def low_lanes(shape):
    return lax.broadcasted_iota(jnp.int32, shape, 1) < 64


def split3(value):
    one = value.astype(BF16)
    rest = value - one.astype(F32)
    two = rest.astype(BF16)
    three = (rest - two.astype(F32)).astype(BF16)
    return one, two, three


def pack_rows(value):
    half = value.shape[0] // 2
    return jnp.where(low_lanes((half, 128)), value[:half], value[half:])


def bits_of(words):
    shift = lax.broadcasted_iota(jnp.int32, (words.shape[0], 32, words.shape[1]), 1)
    wide = jnp.broadcast_to(words[:, None, :], shift.shape)
    bits = jnp.bitwise_and(jnp.right_shift(wide, shift), 1).astype(F32)
    return bits.reshape(words.shape[0] * 32, words.shape[1])


def local_gram(packed):
    full = dot(packed, packed, (0, 0), HIGHEST)
    gram = full[:64] + swap(full[64:])
    return jnp.where(low_lanes((32, 128)), gram[:32], swap(gram[32:]))


def inverse_factor(gram):
    size = 64
    rows = lax.broadcasted_iota(jnp.int32, (size, 128), 0)
    lanes = lax.broadcasted_iota(jnp.int32, (size, 128), 1)
    low = lanes < size
    square = jnp.concatenate([gram, swap(gram)], axis=0)
    work = jnp.where(low, square, (lanes - size == rows).astype(F32))
    done = []
    for j in range(size):
        start = (j // 8) * 8
        top = j - start
        row = work[top : top + 1, :]
        column = jnp.broadcast_to(work[:, j : j + 1], work.shape)
        pivot = 1.0 / column[top : top + 1, :]
        index = lax.broadcasted_iota(jnp.int32, work.shape, 0) + start
        work = work - jnp.where(index > j, column, 0.0) * (pivot * row)
        if top == 7:
            done.append(work[:8])
            work = work[8:]
    work = jnp.concatenate(done, axis=0)
    diag = jnp.sum(jnp.where(lanes == rows, work, 0.0), axis=1, keepdims=True)
    inverse = work * (1.0 / jnp.sqrt(diag))
    return jnp.concatenate(
        [jnp.where(low, swap(inverse), 0.0), jnp.where(low, 0.0, inverse)], axis=0
    )


def kernel(
    lines, inner, rows, words_ref, start_ref, out_ref,
    words_i, words_j, block0, block1, kern, terms, stacked,
    row_parts, col_parts, send1, send2, part1, part2, gram1, gram2, gram3,
    send_sem, recv_sem,
):
    me = lax.axis_index("row")
    mine_a = me // inner
    mine_b = me % inner
    width = lines * rows
    half = rows // 2

    def inner_peer(step):
        slot = lax.rem(mine_b + step, inner)
        return slot, mine_a * inner + slot

    def line_peer(step):
        slot = lax.rem(mine_a + step, lines)
        return slot, slot * inner + mine_b

    barrier = pltpu.get_barrier_semaphore()
    for step in range(1, inner):
        pl.semaphore_signal(barrier, 1, device_id={"row": inner_peer(step)[1]}, device_id_type=MESH)
    for step in range(1, lines):
        pl.semaphore_signal(barrier, 1, device_id={"row": line_peer(step)[1]}, device_id_type=MESH)

    count = [0]
    started = []

    def exchange(size, peer, mine, buffer):
        waits = []
        for step in range(1, size):
            index = count[0]
            count[0] += 1
            target = peer(step)[1]
            copy = pltpu.make_async_remote_copy(
                src_ref=buffer.at[mine], dst_ref=buffer.at[mine],
                send_sem=send_sem.at[index], recv_sem=recv_sem.at[index],
                device_id={"row": target}, device_id_type=MESH,
            )
            copy.start()
            started.append(copy)
            slot = peer(size - step)[0]
            waits.append(
                pltpu.make_async_remote_copy(
                    src_ref=buffer.at[slot], dst_ref=buffer.at[slot],
                    send_sem=send_sem.at[index], recv_sem=recv_sem.at[index],
                    device_id={"row": target}, device_id_type=MESH,
                )
            )
        return waits

    def finish(waits):
        for copy in waits:
            copy.wait_recv()

    words_i[mine_b] = words_ref[...]
    words_j[mine_a] = words_ref[...]
    start = start_ref[...]
    block0[mine_a] = jnp.concatenate([start[:half], start[half:]], axis=1)

    pl.semaphore_wait(barrier, inner + lines - 2)
    wait_j = exchange(lines, line_peer, mine_a, words_j)
    wait_i = exchange(inner, inner_peer, mine_b, words_i)
    wait_x = exchange(lines, line_peer, mine_a, block0)

    finish(wait_j)
    right = bits_of(jnp.concatenate([words_j[d] for d in range(lines)], axis=1))
    count_j = jnp.sum(right, axis=0, keepdims=True)
    right = jnp.concatenate(
        [right.astype(BF16), jnp.ones((right.shape[0], 128), BF16)], axis=1
    )
    finish(wait_i)
    col_sum = jnp.zeros((8, width), F32)
    row_list = []
    for q in range(inner):
        left = bits_of(words_i[q]).astype(BF16)
        shared = dot(left, right, (0, 0))
        count_i = jnp.concatenate([shared[:, width:]] * (width // 128), axis=1)
        shared = shared[:, :width]
        tile = shared / (count_i + count_j - shared)
        kern[q * rows : (q + 1) * rows, :] = tile
        col_sum = col_sum + jnp.sum(tile.reshape(rows // 8, 8, width), axis=0)
        lane_sum = tile[:, :128]
        for piece in range(1, width // 128):
            lane_sum = lane_sum + tile[:, piece * 128 : (piece + 1) * 128]
        row_list.append(jnp.sum(lane_sum.T, axis=0, keepdims=True))
    row_parts[mine_b] = jnp.concatenate(row_list, axis=0)
    col_parts[mine_a] = jnp.sum(col_sum, axis=0, keepdims=True)
    wait_r = exchange(inner, inner_peer, mine_b, row_parts)
    wait_c = exchange(lines, line_peer, mine_a, col_parts)

    low = low_lanes((half, 128))

    def fill(block):
        for d in range(lines):
            one, two, three = [t.astype(F32) for t in split3(block[d])]
            base = d * rows
            stacked[base : base + half, :] = jnp.concatenate(
                [jnp.where(low, one, swap(two)), jnp.where(low, three, 0.0)], axis=1
            ).astype(BF16)
            stacked[base + half : base + rows, :] = jnp.concatenate(
                [jnp.where(low, swap(one), two), jnp.where(low, swap(three), 0.0)], axis=1
            ).astype(BF16)

    def fold(wide):
        both = wide[:, :128] + wide[:, 128:]
        return both + swap(both)

    finish(wait_x)
    fill(block0)

    finish(wait_r + wait_c)
    degree_i = row_parts[0]
    for q in range(1, inner):
        degree_i = degree_i + row_parts[q]
    degree_j = col_parts[0]
    for d in range(1, lines):
        degree_j = degree_j + col_parts[d]
    root_j = jnp.sqrt(degree_j)
    inv_j = 1.0 / root_j
    volume_part = jnp.sum(degree_j)
    own = jnp.zeros((1, rows), F32)
    for q in range(inner):
        own = own + jnp.where(mine_b == q, degree_i[q : q + 1], 0.0)
        column = jnp.broadcast_to(degree_i[q : q + 1], (128, rows)).T
        inv_i = jnp.concatenate([1.0 / jnp.sqrt(column)] * (width // 128), axis=1)
        span = slice(q * rows, (q + 1) * rows)
        one, two, three = split3(kern[span, :] * inv_i * inv_j)
        terms[0, span, :] = one
        terms[1, span, :] = two
        terms[2, span, :] = three
    own_root = pack_rows(jnp.sqrt(jnp.broadcast_to(own, (128, rows)).T))
    root_terms = jnp.concatenate(
        [t.astype(F32) for t in split3(root_j)] + [jnp.zeros((13, width), F32)], axis=0
    ).astype(BF16)
    first_row = lax.broadcasted_iota(jnp.int32, (8, 128), 0) == 0

    def apply(send, part):
        block = stacked[...]
        proj = jnp.sum(fold(dot(root_terms, block, (1, 0))), axis=0, keepdims=True)
        tail = jnp.where(first_row, jnp.broadcast_to(proj, (8, 128)), volume_part)
        waits = []
        for step in list(range(1, inner)) + [0]:
            slot, target = inner_peer(step)
            span = pl.ds(pl.multiple_of(slot * rows, 32), rows)
            wide = (
                dot(terms[2, span, :], block, (1, 0))
                + dot(terms[1, span, :], block, (1, 0))
                + dot(terms[0, span, :], block, (1, 0))
            )
            place = part.at[mine_b] if step == 0 else send.at[step]
            place[:half, :] = pack_rows(fold(wide))
            place[half:, :] = tail
            if step:
                index = count[0]
                count[0] += 1
                copy = pltpu.make_async_remote_copy(
                    src_ref=send.at[step], dst_ref=part.at[mine_b],
                    send_sem=send_sem.at[index], recv_sem=recv_sem.at[index],
                    device_id={"row": target}, device_id_type=MESH,
                )
                copy.start()
                started.append(copy)
                source = inner_peer(inner - step)[0]
                waits.append(
                    pltpu.make_async_remote_copy(
                        src_ref=send.at[step], dst_ref=part.at[source],
                        send_sem=send_sem.at[index], recv_sem=recv_sem.at[index],
                        device_id={"row": target}, device_id_type=MESH,
                    )
                )
        return waits

    def collect(part):
        total = part[0]
        for q in range(1, inner):
            total = total + part[q]
        proj = total[half : half + 1]
        volume = total[half + 1 : half + 2]
        return total[:half] - own_root * (proj / volume)

    finish(apply(send1, part1))
    block1[mine_a] = collect(part1)
    finish(exchange(lines, line_peer, mine_a, block1))

    gram = local_gram(block1[0])
    for d in range(1, lines):
        gram = gram + local_gram(block1[d])
    gram1[mine_b] = gram
    wait_g = exchange(inner, inner_peer, mine_b, gram1)
    fill(block1)
    wait_y = apply(send2, part2)
    finish(wait_g)
    gram = gram1[0]
    for q in range(1, inner):
        gram = gram + gram1[q]
    factor = inverse_factor(gram)
    finish(wait_y)
    image = dot(collect(part2), factor, (1, 1), HIGHEST)

    gram2[mine_b] = local_gram(image)
    finish(exchange(inner, inner_peer, mine_b, gram2))
    gram = gram2[0]
    for q in range(1, inner):
        gram = gram + gram2[q]
    gram3[mine_a] = gram
    finish(exchange(lines, line_peer, mine_a, gram3))
    gram = gram3[0]
    for d in range(1, lines):
        gram = gram + gram3[d]
    basis = dot(image, inverse_factor(gram), (1, 1), HIGHEST)
    basis = basis * math.sqrt(rows * lines * inner)
    out_ref[:half, :] = basis[:, :64]
    out_ref[half:, :] = basis[:, 64:]
    for copy in started:
        copy.wait_send()


def shards(prints_a, prints_b, prints_c, prints_d, start_block):
    rows, columns = start_block.shape
    devices = lax.axis_size("row")
    inner = 1
    while inner * inner < devices or devices % inner:
        inner += 1
    lines = devices // inner
    words = jnp.concatenate(
        [prints_a.T, prints_b.T, prints_c.T, prints_d.T], axis=0
    )
    depth = words.shape[0]
    copies = 6 * (inner - 1) + 5 * (lines - 1)
    half = rows // 2
    return pl.pallas_call(
        functools.partial(kernel, lines, inner, rows),
        out_shape=jax.ShapeDtypeStruct((rows, columns), F32),
        in_specs=[pl.BlockSpec(memory_space=pltpu.VMEM)] * 2,
        out_specs=pl.BlockSpec(memory_space=pltpu.VMEM),
        scratch_shapes=[
            pltpu.VMEM((inner, depth, rows), jnp.int32),
            pltpu.VMEM((lines, depth, rows), jnp.int32),
            pltpu.VMEM((lines, half, 128), F32),
            pltpu.VMEM((lines, half, 128), F32),
            pltpu.VMEM((inner * rows, lines * rows), F32),
            pltpu.VMEM((3, inner * rows, lines * rows), BF16),
            pltpu.VMEM((lines * rows, 256), BF16),
            pltpu.VMEM((inner, inner, rows), F32),
            pltpu.VMEM((lines, 1, lines * rows), F32),
            pltpu.VMEM((inner, half + 8, 128), F32),
            pltpu.VMEM((inner, half + 8, 128), F32),
            pltpu.VMEM((inner, half + 8, 128), F32),
            pltpu.VMEM((inner, half + 8, 128), F32),
            pltpu.VMEM((inner, 32, 128), F32),
            pltpu.VMEM((inner, 32, 128), F32),
            pltpu.VMEM((lines, 32, 128), F32),
            pltpu.SemaphoreType.DMA((copies,)),
            pltpu.SemaphoreType.DMA((copies,)),
        ],
        compiler_params=pltpu.CompilerParams(
            collective_id=0, has_side_effects=True, vmem_limit_bytes=56 * 2**20
        ),
    )(words, start_block)


def solution(mesh):
    placed = (P(("grp", "row"), None),) * 5
    return jax.shard_map(
        shards, mesh=mesh, in_specs=placed, out_specs=P(("grp", "row"), None), check_vma=False
    )
```

```python
import functools
import math

import jax
import jax.numpy as jnp
from jax import lax
from jax.experimental import pallas as pl
from jax.experimental.pallas import tpu as pltpu
from jax.sharding import PartitionSpec as P

F32 = jnp.float32
BF16 = jnp.bfloat16
HIGHEST = lax.Precision.HIGHEST
MESH = pl.DeviceIdType.MESH


def dot(left, right, dims, precision=None):
    return lax.dot_general(
        left, right, ((dims[:1], dims[1:]), ((), ())),
        precision=precision, preferred_element_type=F32,
    )


def swap(value):
    return pltpu.roll(value, 64, 1)


def low_lanes(shape):
    return lax.broadcasted_iota(jnp.int32, shape, 1) < 64


def split3(value):
    one = value.astype(BF16)
    rest = value - one.astype(F32)
    two = rest.astype(BF16)
    three = (rest - two.astype(F32)).astype(BF16)
    return one, two, three


def pack_rows(value):
    half = value.shape[0] // 2
    return jnp.where(low_lanes((half, 128)), value[:half], value[half:])


def bits_of(words):
    shift = lax.broadcasted_iota(jnp.int32, (words.shape[0], 32, words.shape[1]), 1)
    wide = jnp.broadcast_to(words[:, None, :], shift.shape)
    bits = jnp.bitwise_and(jnp.right_shift(wide, shift), 1).astype(F32)
    return bits.reshape(words.shape[0] * 32, words.shape[1])


def local_gram(packed):
    full = dot(packed, packed, (0, 0), HIGHEST)
    gram = full[:64] + swap(full[64:])
    return jnp.where(low_lanes((32, 128)), gram[:32], swap(gram[32:]))


def inverse_factor(gram):
    size, panels = 64, 8
    rows = lax.broadcasted_iota(jnp.int32, (size, 128), 0)
    lanes = lax.broadcasted_iota(jnp.int32, (size, 128), 1)
    low = lanes < size
    index = lax.broadcasted_iota(jnp.int32, (8, 128), 0)
    square = jnp.concatenate([gram, swap(gram)], axis=0)
    work = jnp.where(low, square, (lanes - size == rows).astype(F32))
    tiles = [work[8 * i : 8 * i + 8] for i in range(panels)]
    for p in range(panels):
        spread = [
            [jnp.broadcast_to(tile[:, k : k + 1], (8, 128)) for k in range(8 * p, 8 * p + 8)]
            for tile in tiles[p:]
        ]
        pivots = jnp.zeros((8, 128), F32)
        for j in range(8):
            head = [jnp.broadcast_to(column[j : j + 1], (8, 128)) for column in spread[0]]
            pivot = 1.0 / head[j]
            pivots = jnp.where(index == j, pivot, pivots)
            line = jnp.broadcast_to(tiles[p][j : j + 1], (8, 128))
            for i in range(p, panels):
                columns = spread[i - p]
                ratio = columns[j] * pivot
                if i == p:
                    ratio = jnp.where(index > j, ratio, 0.0)
                for k in range(j + 1, 8):
                    columns[k] = columns[k] - ratio * head[k]
                tiles[i] = tiles[i] - ratio * line
        tiles[p] = tiles[p] * jnp.sqrt(pivots)
    inverse = jnp.concatenate(tiles, axis=0)
    return jnp.concatenate(
        [jnp.where(low, swap(inverse), 0.0), jnp.where(low, 0.0, inverse)], axis=0
    )


def kernel(
    lines, inner, rows, a_ref, b_ref, c_ref, d_ref, start_ref, out_ref,
    words_i, words_j, block0, block1, kern, terms, stacked,
    row_parts, col_parts, send1, send2, part1, part2, gram1, gram2, gram3,
    send_sem, recv_sem,
):
    me = lax.axis_index("row")
    mine_a = me // inner
    mine_b = me % inner
    width = lines * rows
    half = rows // 2

    def inner_peer(step):
        slot = lax.rem(mine_b + step, inner)
        return slot, mine_a * inner + slot

    def line_peer(step):
        slot = lax.rem(mine_a + step, lines)
        return slot, slot * inner + mine_b

    barrier = pltpu.get_barrier_semaphore()
    for step in range(1, inner):
        pl.semaphore_signal(barrier, 1, device_id={"row": inner_peer(step)[1]}, device_id_type=MESH)
    for step in range(1, lines):
        pl.semaphore_signal(barrier, 1, device_id={"row": line_peer(step)[1]}, device_id_type=MESH)

    count = [0]
    started = []

    def exchange(size, peer, mine, buffer):
        waits = []
        for step in range(1, size):
            index = count[0]
            count[0] += 1
            target = peer(step)[1]
            copy = pltpu.make_async_remote_copy(
                src_ref=buffer.at[mine], dst_ref=buffer.at[mine],
                send_sem=send_sem.at[index], recv_sem=recv_sem.at[index],
                device_id={"row": target}, device_id_type=MESH,
            )
            copy.start()
            started.append(copy)
            slot = peer(size - step)[0]
            waits.append(
                pltpu.make_async_remote_copy(
                    src_ref=buffer.at[slot], dst_ref=buffer.at[slot],
                    send_sem=send_sem.at[index], recv_sem=recv_sem.at[index],
                    device_id={"row": target}, device_id_type=MESH,
                )
            )
        return waits

    def finish(waits):
        for copy in waits:
            copy.wait_recv()

    taken = 0
    for ref in (a_ref, b_ref, c_ref, d_ref):
        words_i[mine_b, taken : taken + ref.shape[0], :] = ref[...]
        words_j[mine_a, taken : taken + ref.shape[0], :] = ref[...]
        taken += ref.shape[0]
    block0[mine_a] = pack_rows(jnp.concatenate([start_ref[...]] * 2, axis=0).T)

    pl.semaphore_wait(barrier, inner + lines - 2)
    wait_j = exchange(lines, line_peer, mine_a, words_j)
    wait_i = exchange(inner, inner_peer, mine_b, words_i)
    wait_x = exchange(lines, line_peer, mine_a, block0)

    finish(wait_j)
    right = bits_of(jnp.concatenate([words_j[d] for d in range(lines)], axis=1))
    count_j = jnp.sum(right, axis=0, keepdims=True)
    right = jnp.concatenate(
        [right.astype(BF16), jnp.ones((right.shape[0], 128), BF16)], axis=1
    )
    finish(wait_i)
    col_sum = jnp.zeros((8, width), F32)
    row_list = []
    for q in range(inner):
        left = bits_of(words_i[q]).astype(BF16)
        shared = dot(left, right, (0, 0))
        count_i = jnp.concatenate([shared[:, width:]] * (width // 128), axis=1)
        shared = shared[:, :width]
        tile = shared / (count_i + count_j - shared)
        kern[q * rows : (q + 1) * rows, :] = tile
        col_sum = col_sum + jnp.sum(tile.reshape(rows // 8, 8, width), axis=0)
        lane_sum = tile[:, :128]
        for piece in range(1, width // 128):
            lane_sum = lane_sum + tile[:, piece * 128 : (piece + 1) * 128]
        row_list.append(jnp.sum(lane_sum.T, axis=0, keepdims=True))
    row_parts[mine_b] = jnp.concatenate(row_list, axis=0)
    col_parts[mine_a] = jnp.sum(col_sum, axis=0, keepdims=True)
    wait_r = exchange(inner, inner_peer, mine_b, row_parts)
    wait_c = exchange(lines, line_peer, mine_a, col_parts)

    low = low_lanes((half, 128))

    def fill(block, slot):
        one, two, three = [t.astype(F32) for t in split3(block[slot])]
        base = slot * rows
        stacked[pl.ds(pl.multiple_of(base, 16), half), :] = jnp.concatenate(
            [jnp.where(low, one, swap(two)), jnp.where(low, three, 0.0)], axis=1
        ).astype(BF16)
        stacked[pl.ds(pl.multiple_of(base + half, 16), half), :] = jnp.concatenate(
            [jnp.where(low, swap(one), two), jnp.where(low, swap(three), 0.0)], axis=1
        ).astype(BF16)

    def fold(wide):
        both = wide[:, :128] + wide[:, 128:]
        return both + swap(both)

    finish(wait_x)
    for d in range(lines):
        fill(block0, d)

    finish(wait_r + wait_c)
    degree_i = row_parts[0]
    for q in range(1, inner):
        degree_i = degree_i + row_parts[q]
    degree_j = col_parts[0]
    for d in range(1, lines):
        degree_j = degree_j + col_parts[d]
    root_j = jnp.sqrt(degree_j)
    inv_j = 1.0 / root_j
    volume_part = jnp.sum(degree_j)
    own = jnp.zeros((1, rows), F32)
    for q in range(inner):
        own = own + jnp.where(mine_b == q, degree_i[q : q + 1], 0.0)
        column = jnp.broadcast_to(degree_i[q : q + 1], (128, rows)).T
        inv_i = jnp.concatenate([1.0 / jnp.sqrt(column)] * (width // 128), axis=1)
        span = slice(q * rows, (q + 1) * rows)
        one, two, three = split3(kern[span, :] * inv_i * inv_j)
        terms[0, span, :] = one
        terms[1, span, :] = two
        terms[2, span, :] = three
    own_root = pack_rows(jnp.sqrt(jnp.broadcast_to(own, (128, rows)).T))
    root_terms = jnp.concatenate(
        [t.astype(F32) for t in split3(root_j)] + [jnp.zeros((13, width), F32)], axis=0
    ).astype(BF16)
    first_row = lax.broadcasted_iota(jnp.int32, (8, 128), 0) == 0

    def apply(send, part):
        block = stacked[...]
        proj = jnp.sum(fold(dot(root_terms, block, (1, 0))), axis=0, keepdims=True)
        tail = jnp.where(first_row, jnp.broadcast_to(proj, (8, 128)), volume_part)
        waits = []
        for step in list(range(1, inner)) + [0]:
            slot, target = inner_peer(step)
            span = pl.ds(pl.multiple_of(slot * rows, 32), rows)
            wide = (
                dot(terms[2, span, :], block, (1, 0))
                + dot(terms[1, span, :], block, (1, 0))
                + dot(terms[0, span, :], block, (1, 0))
            )
            place = part.at[mine_b] if step == 0 else send.at[step]
            place[:half, :] = pack_rows(fold(wide))
            place[half:, :] = tail
            if step:
                index = count[0]
                count[0] += 1
                copy = pltpu.make_async_remote_copy(
                    src_ref=send.at[step], dst_ref=part.at[mine_b],
                    send_sem=send_sem.at[index], recv_sem=recv_sem.at[index],
                    device_id={"row": target}, device_id_type=MESH,
                )
                copy.start()
                started.append(copy)
                source = inner_peer(inner - step)[0]
                waits.append(
                    pltpu.make_async_remote_copy(
                        src_ref=send.at[step], dst_ref=part.at[source],
                        send_sem=send_sem.at[index], recv_sem=recv_sem.at[index],
                        device_id={"row": target}, device_id_type=MESH,
                    )
                )
        return waits

    def collect(part):
        total = part[0]
        for q in range(1, inner):
            total = total + part[q]
        proj = total[half : half + 1]
        volume = total[half + 1 : half + 2]
        return total[:half] - own_root * (proj / volume)

    finish(apply(send1, part1))
    block1[mine_a] = collect(part1)
    wait_x = exchange(lines, line_peer, mine_a, block1)

    gram = local_gram(block1[mine_a])
    fill(block1, mine_a)
    for step in range(1, lines):
        finish(wait_x[step - 1 : step])
        slot = line_peer(lines - step)[0]
        gram = gram + local_gram(block1[slot])
        fill(block1, slot)
    gram1[mine_b] = gram
    wait_g = exchange(inner, inner_peer, mine_b, gram1)
    wait_y = apply(send2, part2)
    finish(wait_g)
    gram = gram1[0]
    for q in range(1, inner):
        gram = gram + gram1[q]
    factor = inverse_factor(gram)
    finish(wait_y)
    image = dot(collect(part2), factor, (1, 1), HIGHEST)

    gram2[mine_b] = local_gram(image)
    finish(exchange(inner, inner_peer, mine_b, gram2))
    gram = gram2[0]
    for q in range(1, inner):
        gram = gram + gram2[q]
    gram3[mine_a] = gram
    finish(exchange(lines, line_peer, mine_a, gram3))
    gram = gram3[0]
    for d in range(1, lines):
        gram = gram + gram3[d]
    basis = dot(image, inverse_factor(gram), (1, 1), HIGHEST)
    basis = basis * math.sqrt(rows * lines * inner)
    out_ref[...] = jnp.concatenate([basis, swap(basis)], axis=0).T[: out_ref.shape[0]]
    for copy in started:
        copy.wait_send()


def shards(prints_a, prints_b, prints_c, prints_d, start_block):
    rows, columns = start_block.shape
    devices = lax.axis_size("row")
    inner = 1
    while inner * inner < devices or devices % inner:
        inner += 1
    lines = devices // inner
    words = [part.T for part in (prints_a, prints_b, prints_c, prints_d)]
    depth = sum(part.shape[0] for part in words)
    copies = 6 * (inner - 1) + 5 * (lines - 1)
    half = rows // 2
    return pl.pallas_call(
        functools.partial(kernel, lines, inner, rows),
        out_shape=jax.ShapeDtypeStruct((columns, rows), F32),
        in_specs=[pl.BlockSpec(memory_space=pltpu.VMEM)] * 5,
        out_specs=pl.BlockSpec(memory_space=pltpu.VMEM),
        scratch_shapes=[
            pltpu.VMEM((inner, depth, rows), jnp.int32),
            pltpu.VMEM((lines, depth, rows), jnp.int32),
            pltpu.VMEM((lines, half, 128), F32),
            pltpu.VMEM((lines, half, 128), F32),
            pltpu.VMEM((inner * rows, lines * rows), F32),
            pltpu.VMEM((3, inner * rows, lines * rows), BF16),
            pltpu.VMEM((lines * rows, 256), BF16),
            pltpu.VMEM((inner, inner, rows), F32),
            pltpu.VMEM((lines, 1, lines * rows), F32),
            pltpu.VMEM((inner, half + 8, 128), F32),
            pltpu.VMEM((inner, half + 8, 128), F32),
            pltpu.VMEM((inner, half + 8, 128), F32),
            pltpu.VMEM((inner, half + 8, 128), F32),
            pltpu.VMEM((inner, 32, 128), F32),
            pltpu.VMEM((inner, 32, 128), F32),
            pltpu.VMEM((lines, 32, 128), F32),
            pltpu.SemaphoreType.DMA((copies,)),
            pltpu.SemaphoreType.DMA((copies,)),
        ],
        compiler_params=pltpu.CompilerParams(
            collective_id=0, has_side_effects=True, vmem_limit_bytes=56 * 2**20
        ),
    )(*words, start_block.T).T


def solution(mesh):
    placed = (P(("grp", "row"), None),) * 5
    return jax.shard_map(
        shards, mesh=mesh, in_specs=placed, out_specs=P(("grp", "row"), None), check_vma=False
    )
```

```python
import functools
import math

import jax
import jax.numpy as jnp
from jax import lax
from jax.experimental import pallas as pl
from jax.experimental.pallas import tpu as pltpu
from jax.sharding import PartitionSpec as P

F32 = jnp.float32
BF16 = jnp.bfloat16
HIGHEST = lax.Precision.HIGHEST
MESH = pl.DeviceIdType.MESH


def dot(left, right, dims, precision=None):
    return lax.dot_general(
        left, right, ((dims[:1], dims[1:]), ((), ())),
        precision=precision, preferred_element_type=F32,
    )


def swap(value):
    return pltpu.roll(value, 64, 1)


def low_lanes(shape):
    return lax.broadcasted_iota(jnp.int32, shape, 1) < 64


def split3(value):
    one = value.astype(BF16)
    rest = value - one.astype(F32)
    two = rest.astype(BF16)
    three = (rest - two.astype(F32)).astype(BF16)
    return one, two, three


def pack_rows(value):
    half = value.shape[0] // 2
    return jnp.where(low_lanes((half, 128)), value[:half], value[half:])


def bits_of(words):
    shift = lax.broadcasted_iota(jnp.int32, (words.shape[0], 32, words.shape[1]), 1)
    wide = jnp.broadcast_to(words[:, None, :], shift.shape)
    bits = jnp.bitwise_and(jnp.right_shift(wide, shift), 1).astype(F32)
    return bits.reshape(words.shape[0] * 32, words.shape[1])


def local_gram(packed):
    full = dot(packed, packed, (0, 0), HIGHEST)
    gram = full[:64] + swap(full[64:])
    return jnp.where(low_lanes((32, 128)), gram[:32], swap(gram[32:]))


def inverse_factor(gram):
    size, panels = 64, 8
    rows = lax.broadcasted_iota(jnp.int32, (size, 128), 0)
    lanes = lax.broadcasted_iota(jnp.int32, (size, 128), 1)
    low = lanes < size
    index = lax.broadcasted_iota(jnp.int32, (8, 128), 0)
    square = jnp.concatenate([gram, swap(gram)], axis=0)
    work = jnp.where(low, square, (lanes - size == rows).astype(F32))
    tiles = [work[8 * i : 8 * i + 8] for i in range(panels)]
    for p in range(panels):
        spread = [
            [jnp.broadcast_to(tile[:, k : k + 1], (8, 128)) for k in range(8 * p, 8 * p + 8)]
            for tile in tiles[p:]
        ]
        pivots = jnp.zeros((8, 128), F32)
        for j in range(8):
            head = [jnp.broadcast_to(column[j : j + 1], (8, 128)) for column in spread[0]]
            pivot = 1.0 / head[j]
            pivots = jnp.where(index == j, pivot, pivots)
            line = jnp.broadcast_to(tiles[p][j : j + 1], (8, 128))
            for i in range(p, panels):
                columns = spread[i - p]
                ratio = columns[j] * pivot
                if i == p:
                    ratio = jnp.where(index > j, ratio, 0.0)
                for k in range(j + 1, 8):
                    columns[k] = columns[k] - ratio * head[k]
                tiles[i] = tiles[i] - ratio * line
        tiles[p] = tiles[p] * jnp.sqrt(pivots)
    inverse = jnp.concatenate(tiles, axis=0)
    return jnp.concatenate(
        [jnp.where(low, swap(inverse), 0.0), jnp.where(low, 0.0, inverse)], axis=0
    )


def kernel(
    lines, inner, rows, a_hbm, b_hbm, c_hbm, d_hbm, start_hbm, image_ref, gram_ref,
    words_i, words_j, block0, block1, kern, terms, stacked,
    row_parts, col_parts, send1, send2, part1, part2, gram1, gram2, gram3,
    send_sem, recv_sem, load_sem, a_ref, b_ref, c_ref, d_ref, start_ref,
):
    me = lax.axis_index("row")
    mine_a = me // inner
    mine_b = me % inner
    width = lines * rows
    half = rows // 2

    def inner_peer(step):
        slot = lax.rem(mine_b + step, inner)
        return slot, mine_a * inner + slot

    def line_peer(step):
        slot = lax.rem(mine_a + step, lines)
        return slot, slot * inner + mine_b

    barrier = pltpu.get_barrier_semaphore()
    for step in range(1, inner):
        pl.semaphore_signal(barrier, 1, device_id={"row": inner_peer(step)[1]}, device_id_type=MESH)
    for step in range(1, lines):
        pl.semaphore_signal(barrier, 1, device_id={"row": line_peer(step)[1]}, device_id_type=MESH)

    loads = [
        pltpu.make_async_copy(source, target, load_sem.at[place])
        for place, (source, target) in enumerate([
            (a_hbm, a_ref), (b_hbm, b_ref), (c_hbm, c_ref), (d_hbm, d_ref), (start_hbm, start_ref)
        ])
    ]
    for load in loads:
        load.start()

    count = [0]
    started = []

    def exchange(size, peer, mine, buffer):
        waits = []
        for step in range(1, size):
            index = count[0]
            count[0] += 1
            target = peer(step)[1]
            copy = pltpu.make_async_remote_copy(
                src_ref=buffer.at[mine], dst_ref=buffer.at[mine],
                send_sem=send_sem.at[index], recv_sem=recv_sem.at[index],
                device_id={"row": target}, device_id_type=MESH,
            )
            copy.start()
            started.append(copy)
            slot = peer(size - step)[0]
            waits.append(
                pltpu.make_async_remote_copy(
                    src_ref=buffer.at[slot], dst_ref=buffer.at[slot],
                    send_sem=send_sem.at[index], recv_sem=recv_sem.at[index],
                    device_id={"row": target}, device_id_type=MESH,
                )
            )
        return waits

    def finish(waits):
        for copy in waits:
            copy.wait_recv()

    for load in loads:
        load.wait()
    taken = 0
    for ref in (a_ref, b_ref, c_ref, d_ref):
        words_i[mine_b, taken : taken + ref.shape[0], :] = ref[...]
        words_j[mine_a, taken : taken + ref.shape[0], :] = ref[...]
        taken += ref.shape[0]
    block0[mine_a] = pack_rows(jnp.concatenate([start_ref[...]] * 2, axis=0).T)

    pl.semaphore_wait(barrier, inner + lines - 2)
    wait_j = exchange(lines, line_peer, mine_a, words_j)
    wait_i = exchange(inner, inner_peer, mine_b, words_i)
    wait_x = exchange(lines, line_peer, mine_a, block0)

    finish(wait_j)
    right = bits_of(jnp.concatenate([words_j[d] for d in range(lines)], axis=1))
    count_j = jnp.sum(right, axis=0, keepdims=True)
    right = jnp.concatenate(
        [right.astype(BF16), jnp.ones((right.shape[0], 128), BF16)], axis=1
    )
    finish(wait_i)
    col_sum = jnp.zeros((8, width), F32)
    row_list = []
    for q in range(inner):
        left = bits_of(words_i[q]).astype(BF16)
        shared = dot(left, right, (0, 0))
        count_i = jnp.concatenate([shared[:, width:]] * (width // 128), axis=1)
        shared = shared[:, :width]
        tile = shared / (count_i + count_j - shared)
        kern[q * rows : (q + 1) * rows, :] = tile
        col_sum = col_sum + jnp.sum(tile.reshape(rows // 8, 8, width), axis=0)
        lane_sum = tile[:, :128]
        for piece in range(1, width // 128):
            lane_sum = lane_sum + tile[:, piece * 128 : (piece + 1) * 128]
        row_list.append(jnp.sum(lane_sum.T, axis=0, keepdims=True))
    row_parts[mine_b] = jnp.concatenate(row_list, axis=0)
    col_parts[mine_a] = jnp.sum(col_sum, axis=0, keepdims=True)
    wait_r = exchange(inner, inner_peer, mine_b, row_parts)
    wait_c = exchange(lines, line_peer, mine_a, col_parts)

    low = low_lanes((half, 128))

    def fill(block, slot):
        one, two, three = [t.astype(F32) for t in split3(block[slot])]
        base = slot * rows
        stacked[pl.ds(pl.multiple_of(base, 16), half), :] = jnp.concatenate(
            [jnp.where(low, one, swap(two)), jnp.where(low, three, 0.0)], axis=1
        ).astype(BF16)
        stacked[pl.ds(pl.multiple_of(base + half, 16), half), :] = jnp.concatenate(
            [jnp.where(low, swap(one), two), jnp.where(low, swap(three), 0.0)], axis=1
        ).astype(BF16)

    def fold(wide):
        both = wide[:, :128] + wide[:, 128:]
        return both + swap(both)

    finish(wait_x)
    for d in range(lines):
        fill(block0, d)

    finish(wait_r + wait_c)
    degree_i = row_parts[0]
    for q in range(1, inner):
        degree_i = degree_i + row_parts[q]
    degree_j = col_parts[0]
    for d in range(1, lines):
        degree_j = degree_j + col_parts[d]
    root_j = jnp.sqrt(degree_j)
    inv_j = 1.0 / root_j
    volume_part = jnp.sum(degree_j)
    own = jnp.zeros((1, rows), F32)
    for q in range(inner):
        own = own + jnp.where(mine_b == q, degree_i[q : q + 1], 0.0)
        column = jnp.broadcast_to(degree_i[q : q + 1], (128, rows)).T
        inv_i = jnp.concatenate([1.0 / jnp.sqrt(column)] * (width // 128), axis=1)
        span = slice(q * rows, (q + 1) * rows)
        one, two, three = split3(kern[span, :] * inv_i * inv_j)
        terms[0, span, :] = one
        terms[1, span, :] = two
        terms[2, span, :] = three
    own_root = pack_rows(jnp.sqrt(jnp.broadcast_to(own, (128, rows)).T))
    root_terms = jnp.concatenate(
        [t.astype(F32) for t in split3(root_j)] + [jnp.zeros((13, width), F32)], axis=0
    ).astype(BF16)
    first_row = lax.broadcasted_iota(jnp.int32, (8, 128), 0) == 0

    def apply(send, part):
        block = stacked[...]
        proj = jnp.sum(fold(dot(root_terms, block, (1, 0))), axis=0, keepdims=True)
        tail = jnp.where(first_row, jnp.broadcast_to(proj, (8, 128)), volume_part)
        waits = []
        for step in list(range(1, inner)) + [0]:
            slot, target = inner_peer(step)
            span = pl.ds(pl.multiple_of(slot * rows, 32), rows)
            wide = (
                dot(terms[2, span, :], block, (1, 0))
                + dot(terms[1, span, :], block, (1, 0))
                + dot(terms[0, span, :], block, (1, 0))
            )
            place = part.at[mine_b] if step == 0 else send.at[step]
            place[:half, :] = pack_rows(fold(wide))
            place[half:, :] = tail
            if step:
                index = count[0]
                count[0] += 1
                copy = pltpu.make_async_remote_copy(
                    src_ref=send.at[step], dst_ref=part.at[mine_b],
                    send_sem=send_sem.at[index], recv_sem=recv_sem.at[index],
                    device_id={"row": target}, device_id_type=MESH,
                )
                copy.start()
                started.append(copy)
                source = inner_peer(inner - step)[0]
                waits.append(
                    pltpu.make_async_remote_copy(
                        src_ref=send.at[step], dst_ref=part.at[source],
                        send_sem=send_sem.at[index], recv_sem=recv_sem.at[index],
                        device_id={"row": target}, device_id_type=MESH,
                    )
                )
        return waits

    def collect(part):
        total = part[0]
        for q in range(1, inner):
            total = total + part[q]
        proj = total[half : half + 1]
        volume = total[half + 1 : half + 2]
        return total[:half] - own_root * (proj / volume)

    finish(apply(send1, part1))
    block1[mine_a] = collect(part1)
    wait_x = exchange(lines, line_peer, mine_a, block1)

    gram = local_gram(block1[mine_a])
    fill(block1, mine_a)
    for step in range(1, lines):
        finish(wait_x[step - 1 : step])
        slot = line_peer(lines - step)[0]
        gram = gram + local_gram(block1[slot])
        fill(block1, slot)
    gram1[mine_b] = gram
    wait_g = exchange(inner, inner_peer, mine_b, gram1)
    wait_y = apply(send2, part2)
    finish(wait_g)
    gram = gram1[0]
    for q in range(1, inner):
        gram = gram + gram1[q]
    factor = inverse_factor(gram)
    finish(wait_y)
    image = dot(collect(part2), factor, (1, 1), HIGHEST)

    gram2[mine_b] = local_gram(image)
    finish(exchange(inner, inner_peer, mine_b, gram2))
    gram = gram2[0]
    for q in range(1, inner):
        gram = gram + gram2[q]
    gram3[mine_a] = gram
    finish(exchange(lines, line_peer, mine_a, gram3))
    gram = gram3[0]
    for d in range(1, lines):
        gram = gram + gram3[d]
    image_ref[...] = image
    gram_ref[...] = gram
    for copy in started:
        copy.wait_send()


def last_kernel(molecules, image_ref, gram_ref, out_ref):
    basis = dot(image_ref[...], inverse_factor(gram_ref[...]), (1, 1), HIGHEST)
    basis = basis * math.sqrt(molecules)
    out_ref[...] = jnp.concatenate([basis, swap(basis)], axis=0).T[: out_ref.shape[0]]


def shards(prints_a, prints_b, prints_c, prints_d, start_block):
    rows, columns = start_block.shape
    devices = lax.axis_size("row")
    inner = 1
    while inner * inner < devices or devices % inner:
        inner += 1
    lines = devices // inner
    words = [part.T for part in (prints_a, prints_b, prints_c, prints_d)]
    depth = sum(part.shape[0] for part in words)
    copies = 6 * (inner - 1) + 5 * (lines - 1)
    half = rows // 2
    image, gram = pl.pallas_call(
        functools.partial(kernel, lines, inner, rows),
        out_shape=(
            jax.ShapeDtypeStruct((half, 128), F32), jax.ShapeDtypeStruct((32, 128), F32)
        ),
        in_specs=[pl.BlockSpec(memory_space=pl.ANY)] * 5,
        out_specs=(pl.BlockSpec(memory_space=pltpu.VMEM),) * 2,
        scratch_shapes=[
            pltpu.VMEM((inner, depth, rows), jnp.int32),
            pltpu.VMEM((lines, depth, rows), jnp.int32),
            pltpu.VMEM((lines, half, 128), F32),
            pltpu.VMEM((lines, half, 128), F32),
            pltpu.VMEM((inner * rows, lines * rows), F32),
            pltpu.VMEM((3, inner * rows, lines * rows), BF16),
            pltpu.VMEM((lines * rows, 256), BF16),
            pltpu.VMEM((inner, inner, rows), F32),
            pltpu.VMEM((lines, 1, lines * rows), F32),
            pltpu.VMEM((inner, half + 8, 128), F32),
            pltpu.VMEM((inner, half + 8, 128), F32),
            pltpu.VMEM((inner, half + 8, 128), F32),
            pltpu.VMEM((inner, half + 8, 128), F32),
            pltpu.VMEM((inner, 32, 128), F32),
            pltpu.VMEM((inner, 32, 128), F32),
            pltpu.VMEM((lines, 32, 128), F32),
            pltpu.SemaphoreType.DMA((copies,)),
            pltpu.SemaphoreType.DMA((copies,)),
            pltpu.SemaphoreType.DMA((5,)),
        ]
        + [pltpu.VMEM(part.shape, jnp.int32) for part in words]
        + [pltpu.VMEM((columns, rows), F32)],
        compiler_params=pltpu.CompilerParams(
            collective_id=0, has_side_effects=True, vmem_limit_bytes=56 * 2**20
        ),
    )(*words, start_block.T)
    return pl.pallas_call(
        functools.partial(last_kernel, rows * devices),
        out_shape=jax.ShapeDtypeStruct((columns, rows), F32),
        in_specs=[pl.BlockSpec(memory_space=pltpu.VMEM)] * 2,
        out_specs=pl.BlockSpec(memory_space=pltpu.VMEM),
    )(image, gram).T


def solution(mesh):
    placed = (P(("grp", "row"), None),) * 5
    return jax.shard_map(
        shards, mesh=mesh, in_specs=placed, out_specs=P(("grp", "row"), None), check_vma=False
    )
```
